32 devices in a mesh: groups: 2 (over y), ex: 4 (over x, core), feat: 4 (over z).
Axes of the slice: x: 2, y: 2, z: 4, core: 2. Of those that a mesh axis runs over, the one named last changes fastest.
Arguments:
- slab: float32 [65536, 1024], P(('groups', 'ex'), 'feat'), parts along dimension 0, may hold values from -150 to 150
- queries: float32 [1024, 1024], P(('groups', 'ex'), 'feat'), parts along dimension 0, may hold values from -6 to 6
- plan: int32 [8, 4], P('groups'), parts along dimension 0, may hold values 0 or 1
- example_ids: int32 [65536], P(('groups', 'ex', 'feat')), parts along dimension 0, may hold values from 0 to 32767
- retain: float32 [65536], P('groups'), parts along dimension 0, may hold values from 0.1 to 1
Outputs:
- scores: float32 [65536, 4, 128], P(('groups', 'ex', 'feat')), parts along dimension 0
The draws below stay inside these ranges and needn't reach their ends.
There are 2 independent parts, one for each index of `groups`. The reference program is written for one: setup_inputs(seed, part) draws one part's arguments, and reference() takes and returns one part's arrays. A program takes and returns all parts, laid end to end along the dimension named above; each array names one. Nothing has to cross between parts.
All inputs are finite; a program needn't handle non-finite values.
Results may differ from the reference program's by a relative error of at most 0.0003.
Values sent between devices are 32-bit elements; how exact they have to be, the bound alone decides.
A program may use at most 128 MiB of HBM per device.

```python
import math
import jax
import jax.numpy as jnp
from jax import lax

P_SIZE = 1024
ROWS = 8192
QBLK = 128
STEPS = 4
NQB = 4
EXAMPLES = 32768
NQ = 512
N_EX = 4


def draw_slab(key, part):
    key = jax.random.fold_in(key, 11)
    keys = jax.random.split(key, 3)
    row_scale = jnp.exp(jax.random.uniform(keys[0], (EXAMPLES, 1), jnp.float32, math.log(0.5), math.log(5.0)))
    col_scale = jnp.exp(jax.random.uniform(keys[1], (1, P_SIZE), jnp.float32, math.log(0.5), math.log(5.0)))
    values = jnp.clip(jax.random.normal(keys[2], (EXAMPLES, P_SIZE), jnp.float32), -6.0, 6.0)
    return row_scale * col_scale * values


def place_ends(result, stream_key, smallest, high):
    longest = result.shape.index(max(result.shape))
    spots = []
    for shift in (0, 1):
        where = [jax.random.randint(jax.random.fold_in(stream_key, axis), (), 0, length) for axis, length in enumerate(result.shape)]
        where[longest] = (where[longest] + shift) % result.shape[longest]
        spots.append(tuple(where))
    return result.at[spots[0]].set(smallest).at[spots[1]].set(high)


def levels(key, dims, cuts, smallest, largest):
    def one(position, blocks):
        draws = jax.random.uniform(jax.random.fold_in(jax.random.fold_in(key, 6), position), (blocks,), jnp.float32, smallest / len(cuts), largest / len(cuts))
        return jnp.repeat(jnp.exp(draws), dims[position] // blocks).reshape((-1,) + (1,) * (len(dims) - position - 1))

    loudness = one(*cuts[0])
    for cut in cuts[1:]:
        loudness = loudness * one(*cut)
    return loudness


def scatter_about(own_key, shape, spread, limit, pieces=(), kind=jnp.bfloat16):
    array = jax.random.normal(own_key, shape, jnp.float32) * spread
    if len(pieces) > 0:
        array = levels(own_key, shape, pieces, -0.22, 0.18) * array
    return jnp.clip(array, min=-limit, max=limit).astype(kind)


def setup_inputs(seed: int = 0, part: int = 0) -> dict:
    splits = jax.random.split(jax.random.key(seed), 6)
    own_keys = jax.random.split(jax.random.fold_in(splits[5], part), 6)
    slab = draw_slab(jax.random.fold_in(jax.random.fold_in(splits[5], part), 71), part)
    queries = scatter_about(own_keys[1], (NQ, P_SIZE), 1.0, 6.0, ((0, 4), (1, 4)), jnp.float32)
    plan = place_ends((jax.random.randint(own_keys[2], (NQB, STEPS), 0, 4) < 3).astype(jnp.int32), jax.random.fold_in(own_keys[2], 1), 0, 1)
    example_ids = place_ends(jax.random.randint(own_keys[3], (EXAMPLES,), 0, EXAMPLES), jax.random.fold_in(own_keys[3], 1), 0, EXAMPLES - 1).astype(jnp.int32)
    retain = jnp.clip(jnp.exp(jax.random.uniform(own_keys[4], (EXAMPLES,), jnp.float32, math.log(0.1), math.log(1.0))), 0.1, 1.0)
    return {"slab": slab, "queries": queries, "plan": plan, "example_ids": example_ids, "retain": retain}


damping = 0.1
score_gain = 4.0

def precondition(factor, query_rows):
    first = lax.linalg.triangular_solve(factor, query_rows, left_side=False, lower=True, transpose_a=True)
    return lax.linalg.triangular_solve(factor, first, left_side=False, lower=True, transpose_a=False)

def reference(slab, queries, plan, example_ids, retain):
    highest = lax.Precision.HIGHEST
    gram_matrix = lax.dot_general(slab.astype(jnp.float32), slab.astype(jnp.float32), (((0,), (0,)), ((), ())), precision=highest, preferred_element_type=jnp.float32)
    gram_matrix = gram_matrix / EXAMPLES + damping * jnp.eye(P_SIZE, dtype=jnp.float32)
    factor = jnp.linalg.cholesky(gram_matrix)
    solved = precondition(factor, queries)
    weights = retain[example_ids] * (score_gain / math.sqrt(P_SIZE))

    def shard_scores(shard):
        resident = lax.dynamic_slice_in_dim(slab, shard * ROWS, ROWS, 0)
        local_weights = lax.dynamic_slice_in_dim(weights, shard * ROWS, ROWS, 0)
        outputs = []
        for offset in range(STEPS):
            anchor = ((shard - offset) % N_EX).astype(jnp.int32)
            query_block = lax.dynamic_slice_in_dim(solved, anchor * QBLK, QBLK, 0)
            flag = plan[anchor, offset].astype(weights.dtype)
            raw_scores = lax.dot_general(resident.astype(jnp.float32), query_block.astype(jnp.float32), (((1,), (1,)), ((), ())), precision=highest, preferred_element_type=jnp.float32)
            outputs.append(raw_scores * (local_weights * flag)[:, None])
        return jnp.stack(outputs, 1)
    scores = lax.map(shard_scores, jnp.arange(N_EX, dtype=jnp.int32))
    return scores.reshape(EXAMPLES, STEPS, QBLK)
```

```python
import functools
import math

import jax
import jax.numpy as jnp
from jax import lax
from jax.experimental import pallas as pl
from jax.experimental.pallas import tpu as pltpu
from jax.sharding import PartitionSpec as P

P_SIZE = 1024
STEPS = 4
STRIP = 256
BLOCK = 128
TILE = 8
PIVOTS = 4

damping = 0.1
score_gain = 4.0
HIGHEST = lax.Precision.HIGHEST


def shifted(block, axis, distance):
    devices = range(lax.axis_size(axis))
    route = [((i - distance) % len(devices), i) for i in devices]
    return lax.ppermute(block, axis, route)


def inverse_block(tiles):
    lane = lax.broadcasted_iota(jnp.int32, (TILE, BLOCK), 1)
    sub = lax.broadcasted_iota(jnp.int32, (TILE, BLOCK), 0)
    shape = (TILE, BLOCK)
    for j in range(0, BLOCK, PIVOTS):
        tp, jr = j // TILE, j % TILE
        inside = (lane >= j) & (lane < j + PIVOTS)
        cols = [
            [jnp.broadcast_to(tile[:, j + l : j + l + 1], shape) for l in range(PIVOTS)]
            for tile in tiles
        ]
        unit = jnp.where(lane == sub + TILE * tp, 1.0, 0.0)
        base = [
            jnp.where(inside, unit if t == tp else 0.0, tile) for t, tile in enumerate(tiles)
        ]
        rows = [
            jnp.broadcast_to(base[tp][jr + l : jr + l + 1, :], shape) for l in range(PIVOTS)
        ]
        piv = {}
        for i in range(PIVOTS):
            for l in range(i, PIVOTS):
                piv[i, l] = jnp.broadcast_to(cols[tp][l][jr + i : jr + i + 1, :], shape)
                piv[l, i] = piv[i, l]
        for a in range(PIVOTS):
            inv = 1.0 / piv[a, a]
            rows[a] = rows[a] * inv
            for l in range(a + 1, PIVOTS):
                piv[a, l] = piv[a, l] * inv
            for i in range(PIVOTS):
                if i == a:
                    continue
                f = piv[i, a]
                rows[i] = rows[i] - f * rows[a]
                for l in range(a + 1, PIVOTS):
                    piv[i, l] = piv[i, l] - f * piv[a, l]
        new = []
        for t in range(len(tiles)):
            value = base[t]
            for l in range(PIVOTS):
                value = value - cols[t][l] * rows[l]
            if t == tp:
                for l in range(PIVOTS):
                    value = jnp.where(sub == jr + l, rows[l], value)
            new.append(value)
        tiles = new
    return tiles


def dot(a, b):
    return lax.dot_general(
        a, b, (((1,), (0,)), ((), ())), precision=HIGHEST, preferred_element_type=jnp.float32
    )


def solve_kernel(examples, strips_ref, queries_ref, out_ref, gram, lower, pivot_rows, inverse, y):
    size = gram.shape[0]
    starts = []
    start = 0
    for i in range(size // STRIP):
        starts.append(start)
        start += size - i * STRIP
    diag = lax.broadcasted_iota(jnp.int32, (STRIP, STRIP), 0) == lax.broadcasted_iota(
        jnp.int32, (STRIP, STRIP), 1
    )
    for i in range(size // STRIP):
        for j in range(i, size // STRIP):
            at = starts[i] + (j - i) * STRIP
            value = strips_ref[:, at : at + STRIP] / examples
            if i == j:
                value = value + jnp.where(diag, damping, 0.0)
            gram[i * STRIP : (i + 1) * STRIP, j * STRIP : (j + 1) * STRIP] = value
            if i != j:
                gram[j * STRIP : (j + 1) * STRIP, i * STRIP : (i + 1) * STRIP] = value.T
    out_ref[...] = queries_ref[...]
    half = size // 2

    def panel(k, carry):
        here = pl.multiple_of(k * BLOCK, BLOCK)
        tiles = [
            gram[pl.ds(here + TILE * t, TILE), pl.ds(here, BLOCK)] for t in range(BLOCK // TILE)
        ]
        tiles = inverse_block(tiles)
        for t in range(BLOCK // TILE):
            inverse[TILE * t : TILE * (t + 1), :] = tiles[t]
        pivot_rows[...] = gram[pl.ds(here, BLOCK), :]
        qy = dot(out_ref[:, pl.ds(here, BLOCK)], inverse[...])
        y[:, pl.ds(here, BLOCK)] = qy

        def trailing(left):
            out_ref[:, left:] -= dot(qy, pivot_rows[:, left:])

            def chunk(c, carry):
                rows = pl.ds(pl.multiple_of(c * STRIP, STRIP), STRIP)
                m = dot(gram[rows, pl.ds(here, BLOCK)], inverse[...])
                lower[rows, pl.ds(here, BLOCK)] = m
                gram[rows, left:] -= dot(m, pivot_rows[:, left:])
                return carry

            lax.fori_loop((k + 1) // (STRIP // BLOCK), size // STRIP, chunk, 0)

        @pl.when(k < half // BLOCK - 1)
        def _():
            trailing(0)

        @pl.when((k >= half // BLOCK - 1) & (k < size // BLOCK - 1))
        def _():
            trailing(half)

        return carry

    lax.fori_loop(0, size // BLOCK, panel, 0)
    for k in reversed(range(size // BLOCK)):
        lo, hi = k * BLOCK, (k + 1) * BLOCK
        value = y[:, lo:hi]
        if hi < size:
            value = value - dot(out_ref[:, hi:], lower[hi:, lo:hi])
        out_ref[:, lo:hi] = value


def precondition(strips, queries, examples):
    rows, size = queries.shape
    return pl.pallas_call(
        functools.partial(solve_kernel, float(examples)),
        out_shape=jax.ShapeDtypeStruct((rows, size), jnp.float32),
        in_specs=[pl.BlockSpec(memory_space=pltpu.VMEM)] * 2,
        out_specs=pl.BlockSpec(memory_space=pltpu.VMEM),
        scratch_shapes=[
            pltpu.VMEM((size, size), jnp.float32),
            pltpu.VMEM((size, size), jnp.float32),
            pltpu.VMEM((BLOCK, size), jnp.float32),
            pltpu.VMEM((BLOCK, BLOCK), jnp.float32),
            pltpu.VMEM((rows, size), jnp.float32),
        ],
        compiler_params=pltpu.CompilerParams(vmem_limit_bytes=40 * 1024 * 1024),
        name="solve",
    )(strips, queries)


def body(slab, queries, plan, example_ids, retain):
    high = lax.Precision.HIGH
    contract = (((0,), (0,)), ((), ()))
    cycle_size = lax.axis_size("ex")
    position = lax.axis_index("ex")
    home = lax.all_gather(queries, "feat", axis=1, tiled=True)
    visiting = [home] + [shifted(home, "ex", offset) for offset in range(1, STEPS)]
    visiting = jnp.concatenate(visiting, 0)
    resident = lax.all_to_all(slab, "feat", split_axis=0, concat_axis=1, tiled=True)
    strips = [
        lax.dot_general(
            resident[:, i : i + STRIP],
            resident[:, i:],
            contract,
            precision=high,
            preferred_element_type=jnp.float32,
        )
        for i in range(0, P_SIZE, STRIP)
    ]
    strips = lax.psum(jnp.concatenate(strips, 1), ("ex", "feat"))
    examples = slab.shape[0] * cycle_size
    solved = precondition(strips, visiting, examples)
    index_base = jnp.arange(cycle_size, dtype=jnp.int32)
    weights = retain[example_ids] * (score_gain / math.sqrt(P_SIZE))
    flags = []
    for offset in range(STEPS):
        anchor = (position - offset) % cycle_size
        flags.append(jnp.sum(jnp.where(index_base == anchor, plan[:, offset], 0)))
    flags = jnp.stack(flags).astype(jnp.float32)
    raw_scores = lax.dot_general(
        resident,
        solved.reshape(STEPS, -1, P_SIZE),
        (((1,), (2,)), ((), ())),
        precision=high,
        preferred_element_type=jnp.float32,
    )
    return raw_scores * (weights[:, None] * flags[None, :])[:, :, None]


def solution(mesh):
    return jax.shard_map(
        body,
        mesh=mesh,
        in_specs=(
            P(("groups", "ex"), "feat"),
            P(("groups", "ex"), "feat"),
            P("groups", None),
            P(("groups", "ex", "feat")),
            P("groups"),
        ),
        out_specs=P(("groups", "ex", "feat"), None, None),
        check_vma=False,
    )
```

```python
import functools
import math

import jax
import jax.numpy as jnp
from jax import lax
from jax.experimental import pallas as pl
from jax.experimental.pallas import tpu as pltpu
from jax.sharding import PartitionSpec as P

P_SIZE = 1024
STEPS = 4
STRIP = 256
BLOCK = 128
TILE = 8
PIVOTS = 4
CHUNKS = 4

damping = 0.1
score_gain = 4.0
HIGHEST = lax.Precision.HIGHEST


def shifted(block, axis, distance):
    devices = range(lax.axis_size(axis))
    route = [((i - distance) % len(devices), i) for i in devices]
    return lax.ppermute(block, axis, route)


def inverse_block(tiles):
    lane = lax.broadcasted_iota(jnp.int32, (TILE, BLOCK), 1)
    sub = lax.broadcasted_iota(jnp.int32, (TILE, BLOCK), 0)
    shape = (TILE, BLOCK)
    for j in range(0, BLOCK, PIVOTS):
        tp, jr = j // TILE, j % TILE
        inside = (lane >= j) & (lane < j + PIVOTS)
        cols = [
            [jnp.broadcast_to(tile[:, j + l : j + l + 1], shape) for l in range(PIVOTS)]
            for tile in tiles
        ]
        unit = jnp.where(lane == sub + TILE * tp, 1.0, 0.0)
        base = [
            jnp.where(inside, unit if t == tp else 0.0, tile) for t, tile in enumerate(tiles)
        ]
        rows = [
            jnp.broadcast_to(base[tp][jr + l : jr + l + 1, :], shape) for l in range(PIVOTS)
        ]
        piv = {}
        for i in range(PIVOTS):
            for l in range(i, PIVOTS):
                piv[i, l] = jnp.broadcast_to(cols[tp][l][jr + i : jr + i + 1, :], shape)
                piv[l, i] = piv[i, l]
        for a in range(PIVOTS):
            inv = 1.0 / piv[a, a]
            rows[a] = rows[a] * inv
            for l in range(a + 1, PIVOTS):
                piv[a, l] = piv[a, l] * inv
            for i in range(PIVOTS):
                if i == a:
                    continue
                f = piv[i, a]
                rows[i] = rows[i] - f * rows[a]
                for l in range(a + 1, PIVOTS):
                    piv[i, l] = piv[i, l] - f * piv[a, l]
        new = []
        for t in range(len(tiles)):
            value = base[t]
            for l in range(PIVOTS):
                value = value - cols[t][l] * rows[l]
            if t == tp:
                for l in range(PIVOTS):
                    value = jnp.where(sub == jr + l, rows[l], value)
            new.append(value)
        tiles = new
    return tiles


def dot(a, b):
    return lax.dot_general(
        a, b, (((1,), (0,)), ((), ())), precision=HIGHEST, preferred_element_type=jnp.float32
    )


def solve_kernel(examples, strips_ref, queries_ref, out_ref, gram, lower, pivot_rows, inverse, y):
    size = gram.shape[0]
    starts = []
    start = 0
    for i in range(size // STRIP):
        starts.append(start)
        start += size - i * STRIP
    diag = lax.broadcasted_iota(jnp.int32, (STRIP, STRIP), 0) == lax.broadcasted_iota(
        jnp.int32, (STRIP, STRIP), 1
    )
    for i in range(size // STRIP):
        for j in range(i, size // STRIP):
            at = starts[i] + (j - i) * STRIP
            value = strips_ref[:, at : at + STRIP] / examples
            if i == j:
                value = value + jnp.where(diag, damping, 0.0)
            gram[i * STRIP : (i + 1) * STRIP, j * STRIP : (j + 1) * STRIP] = value
            if i != j:
                gram[j * STRIP : (j + 1) * STRIP, i * STRIP : (i + 1) * STRIP] = value.T
    out_ref[...] = queries_ref[...]
    half = size // 2

    def panel(k, carry):
        here = pl.multiple_of(k * BLOCK, BLOCK)
        tiles = [
            gram[pl.ds(here + TILE * t, TILE), pl.ds(here, BLOCK)] for t in range(BLOCK // TILE)
        ]
        tiles = inverse_block(tiles)
        for t in range(BLOCK // TILE):
            inverse[TILE * t : TILE * (t + 1), :] = tiles[t]
        pivot_rows[...] = gram[pl.ds(here, BLOCK), :]
        qy = dot(out_ref[:, pl.ds(here, BLOCK)], inverse[...])
        y[:, pl.ds(here, BLOCK)] = qy

        def trailing(left):
            out_ref[:, left:] -= dot(qy, pivot_rows[:, left:])

            def chunk(c, carry):
                rows = pl.ds(pl.multiple_of(c * STRIP, STRIP), STRIP)
                m = dot(gram[rows, pl.ds(here, BLOCK)], inverse[...])
                lower[rows, pl.ds(here, BLOCK)] = m
                gram[rows, left:] -= dot(m, pivot_rows[:, left:])
                return carry

            lax.fori_loop((k + 1) // (STRIP // BLOCK), size // STRIP, chunk, 0)

        @pl.when(k < half // BLOCK - 1)
        def _():
            trailing(0)

        @pl.when((k >= half // BLOCK - 1) & (k < size // BLOCK - 1))
        def _():
            trailing(half)

        return carry

    lax.fori_loop(0, size // BLOCK, panel, 0)
    for k in reversed(range(size // BLOCK)):
        lo, hi = k * BLOCK, (k + 1) * BLOCK
        value = y[:, lo:hi]
        if hi < size:
            value = value - dot(out_ref[:, hi:], lower[hi:, lo:hi])
        out_ref[:, lo:hi] = value


def precondition(strips, queries, examples):
    rows, size = queries.shape
    return pl.pallas_call(
        functools.partial(solve_kernel, float(examples)),
        out_shape=jax.ShapeDtypeStruct((rows, size), jnp.float32),
        in_specs=[pl.BlockSpec(memory_space=pltpu.VMEM)] * 2,
        out_specs=pl.BlockSpec(memory_space=pltpu.VMEM),
        scratch_shapes=[
            pltpu.VMEM((size, size), jnp.float32),
            pltpu.VMEM((size, size), jnp.float32),
            pltpu.VMEM((BLOCK, size), jnp.float32),
            pltpu.VMEM((BLOCK, BLOCK), jnp.float32),
            pltpu.VMEM((rows, size), jnp.float32),
        ],
        compiler_params=pltpu.CompilerParams(vmem_limit_bytes=40 * 1024 * 1024),
        name="solve",
    )(strips, queries)


def reduce_kernel(strips_ref, out_ref, acc1, buf1, acc2, buf2, buf3, full, send, recv):
    e, f = lax.axis_index("ex"), lax.axis_index("feat")
    depth = lax.axis_size("feat")
    c, x = lax.rem(e, 2), lax.div(e, 2)
    core, across = {"ex": e + 1 - 2 * c}, {"ex": e + 2 - 4 * x}
    peers = [lax.rem(f + d, depth) for d in range(1, depth)]
    barrier = pltpu.get_barrier_semaphore()
    for device in [core, across] + [{"feat": p} for p in peers]:
        pl.semaphore_signal(barrier, inc=1, device_id=device, device_id_type=pl.DeviceIdType.MESH)
    pl.semaphore_wait(barrier, depth + 1)
    rows, columns = strips_ref.shape
    half, quarter, piece = rows // 2, rows // 4, rows // 4 // depth
    width = columns // CHUNKS
    at = lambda start, size: pl.ds(pl.multiple_of(start, size), size)
    mine1 = at(c * half, half)
    mine2 = at(c * half + x * quarter, quarter)
    mine3 = at(c * half + x * quarter + f * piece, piece)
    copies = {}

    def start(ch, name, src, dst, device):
        i = len([1 for key in copies if key[0] == ch])
        copy = pltpu.make_async_remote_copy(
            src_ref=src, dst_ref=dst, send_sem=send.at[ch, i], recv_sem=recv.at[ch, i],
            device_id=device, device_id_type=pl.DeviceIdType.MESH,
        )
        copy.start()
        copies[ch, name] = copy

    def stage(ch, step):
        cols = slice(ch * width, (ch + 1) * width)
        if step == 0:
            away = at((1 - c) * half, half)
            start(ch, "core", strips_ref.at[away, cols], buf1.at[:, cols], core)
        if step == 1:
            copies[ch, "core"].wait_recv()
            acc1[:, cols] = strips_ref[mine1, cols] + buf1[:, cols]
            away = at((1 - x) * quarter, quarter)
            start(ch, "across", acc1.at[away, cols], buf2.at[:, cols], across)
        if step == 2:
            copies[ch, "across"].wait_recv()
            acc2[:, cols] = acc1[at(x * quarter, quarter), cols] + buf2[:, cols]
            for d, p in enumerate(peers):
                src = acc2.at[at(p * piece, piece), cols]
                start(ch, ("in", d), src, buf3.at[d, :, cols], {"feat": p})
        if step == 3:
            value = acc2[at(f * piece, piece), cols]
            for d, p in enumerate(peers):
                copies[ch, ("in", d)].wait_recv()
                value = value + buf3[d, :, cols]
            full[mine3, cols] = value
            for d, p in enumerate(peers):
                start(ch, ("out", d), full.at[mine3, cols], full.at[mine3, cols], {"feat": p})
        if step == 4:
            for d, p in enumerate(peers):
                copies[ch, ("out", d)].wait_recv()
            start(ch, "back", full.at[mine2, cols], full.at[mine2, cols], across)
        if step == 5:
            copies[ch, "back"].wait_recv()
            start(ch, "home", full.at[mine1, cols], full.at[mine1, cols], core)
        if step == 6:
            copies[ch, "home"].wait_recv()
            out_ref[:, cols] = full[:, cols]

    for tick in range(CHUNKS + 6):
        for ch in range(CHUNKS):
            if 0 <= tick - ch <= 6:
                stage(ch, tick - ch)
    for copy in copies.values():
        copy.wait_send()


def summed(strips):
    cycle_size, depth = lax.axis_size("ex"), lax.axis_size("feat")
    rows, columns = strips.shape
    if cycle_size != 4 or rows % (32 * depth):
        return lax.psum(strips, ("ex", "feat"))
    half, quarter, piece = rows // 2, rows // 4, rows // 4 // depth
    count = 4 + 2 * (depth - 1)
    return pl.pallas_call(
        reduce_kernel,
        out_shape=jax.ShapeDtypeStruct(strips.shape, jnp.float32),
        in_specs=[pl.BlockSpec(memory_space=pltpu.VMEM)],
        out_specs=pl.BlockSpec(memory_space=pltpu.VMEM),
        scratch_shapes=[
            pltpu.VMEM((half, columns), jnp.float32),
            pltpu.VMEM((half, columns), jnp.float32),
            pltpu.VMEM((quarter, columns), jnp.float32),
            pltpu.VMEM((quarter, columns), jnp.float32),
            pltpu.VMEM((depth - 1, piece, columns), jnp.float32),
            pltpu.VMEM((rows, columns), jnp.float32),
            pltpu.SemaphoreType.DMA((CHUNKS, count)),
            pltpu.SemaphoreType.DMA((CHUNKS, count)),
        ],
        compiler_params=pltpu.CompilerParams(
            collective_id=0, has_side_effects=True, vmem_limit_bytes=32 * 1024 * 1024
        ),
        name="sum_gram",
    )(strips)


def split(value):
    top = value.astype(jnp.bfloat16)
    return top, (value - top.astype(jnp.float32)).astype(jnp.bfloat16)


def score_kernel(rows_ref, solved_ref, scale_ref, out_ref, top, rest):
    @pl.when(pl.program_id(0) == 0)
    def _():
        top[...], rest[...] = split(solved_ref[...])

    dims = (((1,), (1,)), ((), ()))
    product = functools.partial(
        lax.dot_general, dimension_numbers=dims, preferred_element_type=jnp.float32
    )
    high, low = split(rows_ref[...])
    raw = product(high, top[...]) + (product(high, rest[...]) + product(low, top[...]))
    block = out_ref.shape[2]
    for s in range(out_ref.shape[1]):
        out_ref[:, s, :] = raw[:, s * block : (s + 1) * block] * scale_ref[:, s : s + 1]


def score(resident, solved, scale):
    rows, size = resident.shape
    steps = scale.shape[1]
    count = solved.shape[0]
    tile = 256
    return pl.pallas_call(
        score_kernel,
        grid=(rows // tile,),
        out_shape=jax.ShapeDtypeStruct((rows, steps, count // steps), jnp.float32),
        in_specs=[
            pl.BlockSpec((tile, size), lambda i: (i, 0)),
            pl.BlockSpec((count, size), lambda i: (0, 0)),
            pl.BlockSpec((tile, steps), lambda i: (i, 0)),
        ],
        out_specs=pl.BlockSpec((tile, steps, count // steps), lambda i: (i, 0, 0)),
        scratch_shapes=[
            pltpu.VMEM((count, size), jnp.bfloat16),
            pltpu.VMEM((count, size), jnp.bfloat16),
        ],
        compiler_params=pltpu.CompilerParams(vmem_limit_bytes=32 * 1024 * 1024),
        name="score",
    )(resident, solved, scale)


def body(slab, queries, plan, example_ids, retain):
    high = lax.Precision.HIGH
    contract = (((0,), (0,)), ((), ()))
    cycle_size = lax.axis_size("ex")
    position = lax.axis_index("ex")
    home = lax.all_gather(queries, "feat", axis=1, tiled=True)
    visiting = [home] + [shifted(home, "ex", offset) for offset in range(1, STEPS)]
    visiting = jnp.concatenate(visiting, 0)
    resident = lax.all_to_all(slab, "feat", split_axis=0, concat_axis=1, tiled=True)
    strips = [
        lax.dot_general(
            resident[:, i : i + STRIP],
            resident[:, i:],
            contract,
            precision=high,
            preferred_element_type=jnp.float32,
        )
        for i in range(0, P_SIZE, STRIP)
    ]
    strips = summed(jnp.concatenate(strips, 1))
    examples = slab.shape[0] * cycle_size
    solved = precondition(strips, visiting, examples)
    index_base = jnp.arange(cycle_size, dtype=jnp.int32)
    weights = retain[example_ids] * (score_gain / math.sqrt(P_SIZE))
    flags = []
    for offset in range(STEPS):
        anchor = (position - offset) % cycle_size
        flags.append(jnp.sum(jnp.where(index_base == anchor, plan[:, offset], 0)))
    flags = jnp.stack(flags).astype(jnp.float32)
    return score(resident, solved, weights[:, None] * flags[None, :])


def solution(mesh):
    return jax.shard_map(
        body,
        mesh=mesh,
        in_specs=(
            P(("groups", "ex"), "feat"),
            P(("groups", "ex"), "feat"),
            P("groups", None),
            P(("groups", "ex", "feat")),
            P("groups"),
        ),
        out_specs=P(("groups", "ex", "feat"), None, None),
        check_vma=False,
    )
```
